32 devices in a mesh: dp: 4 (over y, x), ctx: 2 (over core), head: 4 (over z).
Axes of the slice: x: 2, y: 2, z: 4, core: 2. Of those that a mesh axis runs over, the one named last changes fastest.
Arguments:
- hidden: bfloat16 [8192, 768], P(('dp', 'ctx', 'head')), may hold values from -6 to 6
- norm_gain: float32 [768], replicated, may hold values from 0.5 to 1.5
- in_weight: bfloat16 [768, 3352], P(('dp', 'ctx')), may hold values from -0.21875 to 0.21875
- conv_weight: float32 [4, 1792], replicated, may hold values from -1.75 to 1.75
- conv_bias: float32 [1792], replicated, may hold values from -1.5 to 1.5
- dt_bias: float32 [24], replicated, may hold values from -6 to -2.5
- a_log: float32 [24], replicated, may hold values from -4.6 to 1.6
- skip_gain: float32 [24], replicated, may hold values from 0.5 to 2
- gate_gain: float32 [1536], replicated, may hold values from 0.5 to 1.5
- out_weight: bfloat16 [1536, 768], P(('dp', 'ctx')), may hold values from -0.15625 to 0.15625
- cotangent: bfloat16 [8192, 768], P(('dp', 'ctx', 'head')), may hold values from -6 to 6
Outputs:
- output: bfloat16 [8192, 768], P(('dp', 'ctx', 'head'))
- grad_hidden: float32 [8192, 768], P(('dp', 'ctx', 'head'))
- grad_norm_gain: float32 [768], replicated
- grad_in_weight: float32 [768, 3352], P(('dp', 'ctx'))
- grad_conv_weight: float32 [4, 1792], replicated
- grad_conv_bias: float32 [1792], replicated
- grad_dt_bias: float32 [24], replicated
- grad_a_log: float32 [24], replicated
- grad_skip_gain: float32 [24], replicated
- grad_gate_gain: float32 [1536], replicated
- grad_out_weight: float32 [1536, 768], P(('dp', 'ctx'))
The draws below stay inside these ranges and needn't reach their ends.
All inputs are finite; a program needn't handle non-finite values.
Results may differ from the reference program's by a relative error of at most 0.0095.
The reference program's roundings to bfloat16 on the way count: a program that leaves them out, or rounds other values in their place, can miss the bound.
Values may be sent and summed in bfloat16 or wider, within the bound.
A program may use at most 128 MiB of HBM per device.

```python
import jax
import jax.numpy as jnp
from jax import lax

D = 768
HEADS = 24
HEADDIM = 64
STATE = 128
CONV = 4
BLOCK = 256
INNER = 1536
CONV_CH = 1792
PROJ = 3352
LENGTH = 2048
TOKENS = 8192
N_DP = 4


def draw_a_log(key, part):
    key = jax.random.fold_in(key, 7)
    return jax.random.uniform(key, (HEADS,), jnp.float32, -4.6, 1.6)


def spiked(array, key, source, target, shards_of, factor):
    def block_of(position):
        return (jnp.arange(array.shape[position]) // (array.shape[position] // shards_of)).reshape((-1,) + (1,) * (array.ndim - 1 - position))

    one_side = jax.random.permutation(key, shards_of)[block_of(target)]
    second = (block_of(target) + shards_of // 2) % shards_of
    return jnp.where((block_of(source) == one_side) | (block_of(source) == second), factor * array, array)


def block_scale(rng, dims, split, low, top_value):
    factor_of, own = 1.0, jax.random.fold_in(rng, 6)
    for dim, blocks in split:
        steps = jnp.exp(jax.random.uniform(jax.random.fold_in(own, dim), (blocks,), jnp.float32, low / len(split), top_value / len(split)))
        factor_of = factor_of * jnp.repeat(steps, dims[dim] // blocks).reshape([-1 if axis == dim else 1 for axis in range(len(dims))])
    return factor_of


def gaussian(key, dims, width, reach, cuts=(), held_as=jnp.bfloat16):
    drawn = width * jax.random.normal(key, dims, jnp.float32)
    if cuts:
        drawn = drawn * block_scale(key, dims, cuts, -0.22, 0.18)
    return jnp.clip(drawn, -reach, reach).astype(held_as)


def heavy_noise(stream_key, dims, deviation, limit, cuts, heavy, held_as=jnp.bfloat16):
    entries = deviation * jax.random.normal(stream_key, dims, jnp.float32)
    if cuts:
        entries = entries * block_scale(stream_key, dims, cuts, -0.22, 0.18)
    return jnp.clip(spiked(entries, jax.random.fold_in(stream_key, 3), *heavy), -limit, limit).astype(held_as)


def setup_inputs(seed: int = 0) -> dict:
    splits = jax.random.split(jax.random.key(seed), 12)
    hidden = heavy_noise(splits[0], (TOKENS, D), 1.0, 6.0, ((0, 32),), (0, 1, 32, 2.75))
    norm_gain = jnp.clip(1.0 + 0.1 * jax.random.normal(splits[1], (D,), jnp.float32), 0.5, 1.5)
    in_weight = gaussian(splits[2], (D, PROJ), D ** -0.5, 0.21875, ((0, 8),))
    conv_weight = gaussian(splits[3], (CONV, CONV_CH), (3 * CONV) ** -0.5, 1.75, (), jnp.float32)
    conv_bias = gaussian(splits[4], (CONV_CH,), 0.3, 1.5, (), jnp.float32)
    dt_bias = jnp.clip(jax.random.uniform(splits[5], (HEADS,), jnp.float32, -6.0, -2.5), -6.0, -2.5)
    a_log = draw_a_log(jax.random.fold_in(splits[11], 71), 0)
    skip_gain = jnp.clip(jax.random.uniform(splits[7], (HEADS,), jnp.float32, 0.5, 2.0), 0.5, 2.0)
    gate_gain = jnp.clip(1.0 + 0.1 * jax.random.normal(splits[8], (INNER,), jnp.float32), 0.5, 1.5)
    out_weight = gaussian(splits[9], (INNER, D), INNER ** -0.5, 0.15625, ((0, 8),))
    cotangent = gaussian(splits[10], (TOKENS, D), 1.0, 6.0, ((0, 32),))
    return {"hidden": hidden, "norm_gain": norm_gain, "in_weight": in_weight, "conv_weight": conv_weight, "conv_bias": conv_bias, "dt_bias": dt_bias, "a_log": a_log, "skip_gain": skip_gain, "gate_gain": gate_gain, "out_weight": out_weight, "cotangent": cotangent}


@jax.custom_vjp
def low(v):
    return lax.optimization_barrier(v.astype(jnp.bfloat16)).astype(jnp.float32)

@jax.custom_vjp
def low_back(v):
    return v

def low_keep(v):
    return (low(v), None)

def low_pass(kept, grad):
    return (grad,)

def back_keep(v):
    return (v, None)

def back_low(kept, grad):
    return (low(grad),)
low.defvjp(low_keep, low_pass)
low_back.defvjp(back_keep, back_low)
epsilon = 1e-05
highest = lax.Precision.HIGHEST

def rms_scale(values, gain_vec):
    variance = lax.optimization_barrier(jnp.mean(values * values, axis=-1, keepdims=True))
    return values * lax.rsqrt(variance + epsilon) * gain_vec

def block_math(carry_state, pieces):
    inputs, b_rows, c_rows, step_sizes, log_decay = pieces
    cumulative = jnp.cumsum(log_decay, axis=0)
    length = inputs.shape[0]
    row_ids = lax.broadcasted_iota(jnp.int32, (length, length), 0)
    col_ids = lax.broadcasted_iota(jnp.int32, (length, length), 1)
    causal = (col_ids <= row_ids)[None]
    spread = cumulative.T[:, :, None] - cumulative.T[:, None, :]
    safe_spread = jnp.where(causal, spread, jnp.zeros_like(spread))
    decays = jnp.where(causal, jnp.exp(safe_spread), jnp.zeros_like(spread))
    scores = jnp.dot(c_rows, b_rows.T, precision=highest)
    weighted = inputs * step_sizes[:, :, None]
    inner_part = jnp.einsum('hij,jhp->ihp', decays * scores[None], weighted, precision=highest)
    carried = jnp.exp(cumulative)[:, :, None] * jnp.einsum('in,hpn->ihp', c_rows, carry_state, precision=highest)
    last_sum = cumulative[-1]
    tail_decay = jnp.exp(last_sum[None, :] - cumulative)
    new_state = jnp.exp(last_sum)[:, None, None] * carry_state + jnp.einsum('jh,jhp,jn->hpn', tail_decay, weighted, b_rows, precision=highest)
    return (new_state, inner_part + carried)

def reference(hidden, norm_gain, in_weight, conv_weight, conv_bias, dt_bias, a_log, skip_gain, gate_gain, out_weight, cotangent):

    def layer_fn(hidden_f, norm_g, in_f, conv_w, conv_b, bias_dt, rate_log, skip_g, gate_g, out_f):

        def one_sequence(seq_rows):
            normed = rms_scale(seq_rows, norm_g)
            projected = low_back(low(jnp.dot(low(normed), in_f, precision=highest)))
            gate_part = projected[:, :INNER]
            conv_in = projected[:, INNER:INNER + CONV_CH]
            dt_raw = projected[:, INNER + CONV_CH:]
            padded = jnp.concatenate([jnp.zeros((CONV - 1, CONV_CH), conv_in.dtype), conv_in], axis=0)
            conv_out = conv_b + conv_w[0] * padded[0:LENGTH]
            for offset in range(1, CONV):
                conv_out = conv_out + conv_w[offset] * padded[offset:offset + LENGTH]
            activated = low_back(low(jax.nn.silu(conv_out)))
            x_heads = activated[:, :INNER].reshape(LENGTH, HEADS, HEADDIM)
            b_rows = activated[:, INNER:INNER + STATE]
            c_rows = activated[:, INNER + STATE:]
            step_sizes = jax.nn.softplus(dt_raw + bias_dt)
            log_decay = -step_sizes * jnp.exp(rate_log)
            block_count = LENGTH // BLOCK
            pieces = (x_heads.reshape(block_count, BLOCK, HEADS, HEADDIM), b_rows.reshape(block_count, BLOCK, STATE), c_rows.reshape(block_count, BLOCK, STATE), step_sizes.reshape(block_count, BLOCK, HEADS), log_decay.reshape(block_count, BLOCK, HEADS))
            zero_state = jnp.zeros((HEADS, HEADDIM, STATE), x_heads.dtype)
            final_state, outputs = lax.scan(jax.checkpoint(block_math), zero_state, pieces)
            mixer_out = outputs.reshape(LENGTH, HEADS, HEADDIM) + skip_g[None, :, None] * x_heads
            mixer_out = low_back(low(mixer_out.reshape(LENGTH, INNER)))
            gated_normed = rms_scale(mixer_out * jax.nn.silu(gate_part), gate_g)
            return seq_rows + jnp.dot(low(gated_normed), out_f, precision=highest)
        per_seq = lax.map(jax.checkpoint(one_sequence), hidden_f.reshape(N_DP, LENGTH, D))
        return per_seq.reshape(TOKENS, D)
    result, pullback = jax.vjp(layer_fn, hidden.astype(jnp.float32), norm_gain.astype(jnp.float32), in_weight.astype(jnp.float32), conv_weight.astype(jnp.float32), conv_bias.astype(jnp.float32), dt_bias.astype(jnp.float32), a_log.astype(jnp.float32), skip_gain.astype(jnp.float32), gate_gain.astype(jnp.float32), out_weight.astype(jnp.float32))
    gradients = pullback(cotangent.astype(jnp.float32))
    return (result.astype(jnp.bfloat16), gradients[0], gradients[1], gradients[2], gradients[3], gradients[4], gradients[5], gradients[6], gradients[7], gradients[8], gradients[9])
```

```python
import jax
import jax.numpy as jnp
from jax import lax
from jax.experimental import pallas as pl
from jax.experimental.pallas import tpu as pltpu
from jax.sharding import PartitionSpec as P

HEADS = 24
HEADDIM = 64
STATE = 128
CONV = 4
INNER = 1536
CONV_CH = 1792
PAIRS = HEADS // 2
PAIR = 2 * HEADDIM
HALO = 8

epsilon = 1e-05
highest = lax.Precision.HIGHEST
f32 = jnp.float32
bf16 = jnp.bfloat16
WEIGHT_AXES = ("dp", "ctx")
SEQ_AXES = ("ctx", "head")


def dot(a, b, dims=(1, 0), **more):
    return lax.dot_general(
        a, b, (((dims[0],), (dims[1],)), ((), ())), preferred_element_type=f32, **more
    )


def pair_columns(p):
    return slice(p * PAIR, (p + 1) * PAIR)


def low_lanes(rows):
    return lax.broadcasted_iota(jnp.int32, (rows, PAIR), 1) < HEADDIM


def spread_pair(values, p, first):
    return jnp.where(first, values[:, 2 * p : 2 * p + 1], values[:, 2 * p + 1 : 2 * p + 2])


def head_selector():
    rows = lax.broadcasted_iota(jnp.int32, (INNER, 128), 0) // HEADDIM
    cols = lax.broadcasted_iota(jnp.int32, (INNER, 128), 1)
    return (rows == cols).astype(f32)


def call(kernel, outs, *args):
    whole = pl.BlockSpec(memory_space=pltpu.VMEM)
    return pl.pallas_call(
        kernel,
        out_shape=[jax.ShapeDtypeStruct(s, d) for s, d in outs],
        in_specs=[whole] * len(args),
        out_specs=[whole] * len(outs),
        compiler_params=pltpu.CompilerParams(vmem_limit_bytes=48 * 1024 * 1024),
    )(*args)


def state_kernel(act, step, tail, xw_out, xs_out, state_out):
    rows = act.shape[0]
    first = low_lanes(rows)
    step_v, tail_v = step[...], tail[...]
    b_rows = act[:, INNER : INNER + STATE]
    for p in range(PAIRS):
        cols = pair_columns(p)
        weighted = act[:, cols].astype(f32) * spread_pair(step_v, p, first)
        xw_out[:, cols] = weighted.astype(bf16)
        tailed = (weighted * spread_pair(tail_v, p, first)).astype(bf16)
        xs_out[:, cols] = tailed
        state_out[cols, :] = dot(tailed, b_rows, (0, 0)).astype(bf16)


def decay_matrix(cum_v, cum_rows, h, causal):
    spread = cum_v[:, h : h + 1] - cum_rows[h : h + 1, :]
    return jnp.exp(jnp.where(causal, spread, -1e30))


def causal_mask(rows):
    return lax.broadcasted_iota(jnp.int32, (rows, rows), 1) <= lax.broadcasted_iota(
        jnp.int32, (rows, rows), 0
    )


def inner_kernel(act, xw, cum, cum_t, y_out):
    rows = act.shape[0]
    first = low_lanes(rows)
    causal = causal_mask(rows)
    scores = dot(act[:, INNER + STATE :], act[:, INNER : INNER + STATE], (1, 1))
    cum_v, cum_rows = cum[...], cum_t[...]
    for p in range(PAIRS):
        cols = pair_columns(p)
        both = []
        for h in (2 * p, 2 * p + 1):
            weights = (decay_matrix(cum_v, cum_rows, h, causal) * scores).astype(bf16)
            both.append(dot(weights, xw[:, cols]))
        y_out[:, cols] = jnp.where(first, both[0], both[1])


def middle_kernel(
    act, inner, carry, grown, skip, gate, gain, grad_gn,
    gated_low_out, grad_gate_out, g_out, adjoint_out, ggain_out, skip_out, row_out, dc_out,
    gated_s, ystate_s,
):
    rows = act.shape[0]
    first = low_lanes(rows)
    grown_v = grown[...]
    c_rows = act[:, INNER + STATE :]
    square = jnp.zeros((rows, 1), f32)
    inner_product = jnp.zeros((rows, 1), f32)
    for p in range(PAIRS):
        cols = pair_columns(p)
        ystate = dot(c_rows, carry[cols, :], (1, 1)) * spread_pair(grown_v, p, first)
        ystate_s[:, cols] = ystate
        mixer = (inner[:, cols] + ystate + skip[:, cols] * act[:, cols].astype(f32)).astype(bf16)
        gate_f = gate[:, cols].astype(f32)
        gated = mixer.astype(f32) * (gate_f * jax.nn.sigmoid(gate_f))
        gated_s[:, cols] = gated
        g_out[:, cols] = mixer
        square = square + jnp.sum(gated * gated, axis=1, keepdims=True)
        inner_product = inner_product + jnp.sum(
            grad_gn[:, cols] * gain[:, cols] * gated, axis=1, keepdims=True
        )
    scale = lax.rsqrt(square * (1.0 / INNER) + epsilon)
    pull = scale * scale * scale * (inner_product * (1.0 / INNER))
    dc_total = jnp.zeros((rows, STATE), f32)
    row_total = jnp.zeros((rows, 128), f32)
    head_col = lax.broadcasted_iota(jnp.int32, (rows, 128), 1)
    for p in range(PAIRS):
        cols = pair_columns(p)
        gated = gated_s[:, cols]
        normal = gated * scale
        gated_low_out[:, cols] = (normal * gain[:, cols]).astype(bf16)
        grad_n = grad_gn[:, cols]
        ggain_out[:, cols] = jnp.sum(grad_n * normal, axis=0, keepdims=True)
        grad_gated = scale * (grad_n * gain[:, cols]) - pull * gated
        gate_f = gate[:, cols].astype(f32)
        sig = jax.nn.sigmoid(gate_f)
        mixer = g_out[:, cols].astype(f32)
        grad_gate_out[:, cols] = (
            grad_gated * mixer * (sig * (1.0 + gate_f * (1.0 - sig)))
        ).astype(bf16)
        g_low = (grad_gated * (gate_f * sig)).astype(bf16)
        g_out[:, cols] = g_low
        g_f = g_low.astype(f32)
        g_grown = (g_f * spread_pair(grown_v, p, first)).astype(bf16)
        adjoint_out[cols, :] = dot(g_grown, c_rows, (0, 0)).astype(bf16)
        dc_total = dc_total + dot(g_grown, carry[cols, :])
        skip_out[:, cols] = jnp.sum(g_f * act[:, cols].astype(f32), axis=0, keepdims=True)
        term = g_f * ystate_s[:, cols]
        for k in range(2):
            part = jnp.sum(jnp.where(first == (k == 0), term, 0.0), axis=1, keepdims=True)
            row_total = row_total + jnp.where(head_col == 2 * p + k, part, 0.0)
    dc_out[...] = dc_total
    row_out[...] = row_total


def inner_back_kernel(act, xw, g, cum, cum_t, u_out, dbc_out):
    rows = act.shape[0]
    first = low_lanes(rows)
    causal = causal_mask(rows)
    b_rows, c_rows = act[:, INNER : INNER + STATE], act[:, INNER + STATE :]
    scores = dot(c_rows, b_rows, (1, 1))
    cum_v, cum_rows = cum[...], cum_t[...]
    grad_scores = jnp.zeros((rows, rows), f32)
    zero = jnp.zeros((rows, PAIR), bf16)
    for p in range(PAIRS):
        cols = pair_columns(p)
        both = []
        for k in range(2):
            decays = decay_matrix(cum_v, cum_rows, 2 * p + k, causal)
            weights = (decays * scores).astype(bf16)
            both.append(dot(weights, g[:, cols], (0, 0)))
            own = jnp.where(first == (k == 0), g[:, cols], zero)
            grad_scores = grad_scores + decays * dot(own, xw[:, cols], (1, 1))
        u_out[:, cols] = jnp.where(first, both[0], both[1])
    low = grad_scores.astype(bf16)
    dbc_out[:, :STATE] = dot(low, c_rows, (0, 0))
    dbc_out[:, STATE:] = dot(low, b_rows)


def outer_back_kernel(
    act, xw, xs, g, inner, u_inner, adjoint, step, tail, skip, dbc, dc_state,
    grad_act_out, diff_out, col_out, direct_out, term_s, col_s, direct_s,
):
    rows = act.shape[0]
    first = low_lanes(rows)
    step_v, tail_v = step[...], tail[...]
    b_rows = act[:, INNER : INNER + STATE]
    db_total = dbc[:, :STATE]
    for p in range(PAIRS):
        cols = pair_columns(p)
        x_f = act[:, cols].astype(f32)
        g_f = g[:, cols].astype(f32)
        step_b = spread_pair(step_v, p, first)
        u_state = dot(b_rows, adjoint[cols, :], (1, 1)) * spread_pair(tail_v, p, first)
        u_in = u_inner[:, cols]
        u_all = u_in + u_state
        grad_act_out[:, cols] = (step_b * u_all + skip[:, cols] * g_f).astype(bf16)
        term_s[:, cols] = g_f * inner[:, cols] - xw[:, cols].astype(f32) * u_in
        col_s[:, cols] = step_b * x_f * u_state
        direct_s[:, cols] = x_f * u_all
        db_total = db_total + dot(xs[:, cols], adjoint[cols, :])
    grad_act_out[:, INNER : INNER + STATE] = db_total.astype(bf16)
    grad_act_out[:, INNER + STATE :] = (dbc[:, STATE:] + dc_state[...]).astype(bf16)
    selector = head_selector()
    diff_out[...] = dot(term_s[...], selector, precision=highest)
    col_out[...] = dot(col_s[...], selector, precision=highest)
    direct_out[...] = dot(direct_s[...], selector, precision=highest)


def shifted(value, axis, by):
    length = lax.axis_size(axis)
    pairs = [(i, i + by) for i in range(length) if 0 <= i + by < length]
    return lax.ppermute(value, axis, pairs)


def exchange(value):
    return lax.all_to_all(value, SEQ_AXES, split_axis=0, concat_axis=0, tiled=True)


def running(parts, factors, reverse):
    count = parts.shape[0]
    order = range(count - 1, -1, -1) if reverse else range(count)
    state = jnp.zeros(parts.shape[1:], f32)
    kept = [None] * count
    for i in order:
        kept[i] = state.astype(bf16)
        state = factors[i][:, None] * state + parts[i].astype(f32)
    return jnp.stack(kept)


def reduce_weight(part):
    shard = lax.psum_scatter(part.astype(bf16), WEIGHT_AXES, scatter_dimension=0, tiled=True)
    return jnp.sum(lax.all_gather(shard, "head").astype(f32), axis=0)


def body(
    hidden,
    norm_gain,
    in_weight,
    conv_weight,
    conv_bias,
    dt_bias,
    a_log,
    skip_gain,
    gate_gain,
    out_weight,
    cotangent,
):
    rows = hidden.shape[0]
    places = lax.axis_size(SEQ_AXES)
    place = lax.axis_index(SEQ_AXES)
    weight_conv = lax.all_gather(in_weight[:, INNER:], WEIGHT_AXES, axis=0, tiled=True)
    before = shifted(hidden[rows - HALO :], SEQ_AXES, 1)
    weight_gate = lax.all_gather(in_weight[:, :INNER], WEIGHT_AXES, axis=0, tiled=True)
    weight_out = lax.all_gather(out_weight, WEIGHT_AXES, axis=0, tiled=True)

    extended_f = jnp.concatenate([before, hidden], axis=0).astype(f32)
    variance = jnp.mean(extended_f * extended_f, axis=-1, keepdims=True)
    r1 = lax.rsqrt(variance + epsilon)
    normed_ext = (extended_f * r1 * norm_gain).astype(bf16)
    hidden_f, r1, normed_low = extended_f[HALO:], r1[HALO:], normed_ext[HALO:]

    projected = dot(normed_ext, weight_conv).astype(bf16)
    extended = projected[HALO - (CONV - 1) :, :CONV_CH].astype(f32)
    dt_in = projected[HALO:, CONV_CH:].astype(f32) + dt_bias
    conv_out = conv_bias + conv_weight[0] * extended[0:rows]
    for k in range(1, CONV):
        conv_out = conv_out + conv_weight[k] * extended[k : k + rows]
    act = (conv_out * jax.nn.sigmoid(conv_out)).astype(bf16)

    row_ids = lax.broadcasted_iota(jnp.int32, (rows, rows), 0)
    col_ids = lax.broadcasted_iota(jnp.int32, (rows, rows), 1)
    lower = (col_ids <= row_ids).astype(f32)
    rate = jnp.exp(a_log)
    step = jax.nn.softplus(dt_in)
    log_decay = -step * rate
    cum = dot(lower, log_decay, precision=highest)
    last = cum[rows - 1 :]
    tail = jnp.exp(last - cum)
    grown = jnp.exp(cum)
    cum_t = cum.T
    skip_wide = jnp.repeat(skip_gain, HEADDIM)[None]

    xw, xs, state = call(
        state_kernel,
        [((rows, INNER), bf16), ((rows, INNER), bf16), ((INNER, STATE), bf16)],
        act, step, tail,
    )
    share = INNER // places
    high = last.astype(bf16)
    rest = last - high.astype(f32)
    middle = rest.astype(bf16)
    lowest = (rest - middle.astype(f32)).astype(bf16)
    logs = jnp.pad(jnp.concatenate([high, middle, lowest], axis=0), ((0, 13), (0, STATE - HEADS)))
    sent = jnp.concatenate(
        [state.reshape(places, share, STATE), jnp.broadcast_to(logs, (places, 16, STATE))], axis=1
    )
    arrived = exchange(sent)
    inner = call(inner_kernel, [((rows, INNER), f32)], act, xw, cum, cum_t)[0]
    gate = dot(normed_low, weight_gate).astype(bf16)
    grad_gn = dot(cotangent, weight_out, (1, 1))

    all_logs = jnp.sum(arrived[:, share : share + 3, :HEADS].astype(f32), axis=1)
    owner = (place * share + jnp.arange(share)) // HEADDIM
    mine = (owner[None] == jnp.arange(HEADS)[:, None]).astype(f32)
    factors = dot(jnp.exp(all_logs), mine, precision=highest)
    carry = exchange(running(arrived[:, :share], factors, False)).reshape(INNER, STATE)

    middle_outs = [
        ((rows, INNER), bf16),
        ((rows, INNER), bf16),
        ((rows, INNER), bf16),
        ((INNER, STATE), bf16),
        ((1, INNER), f32),
        ((1, INNER), f32),
        ((rows, 128), f32),
        ((rows, STATE), f32),
    ]
    whole = pl.BlockSpec(memory_space=pltpu.VMEM)
    gated_low, grad_gate, g, adjoint_part, ggain, gskip, row_state, dc_state = pl.pallas_call(
        middle_kernel,
        out_shape=[jax.ShapeDtypeStruct(s, d) for s, d in middle_outs],
        in_specs=[whole] * 8,
        out_specs=[whole] * 8,
        scratch_shapes=[pltpu.VMEM((rows, INNER), f32)] * 2,
        compiler_params=pltpu.CompilerParams(vmem_limit_bytes=48 * 1024 * 1024),
    )(act, inner, carry, grown, skip_wide, gate, gate_gain[None], grad_gn)

    arrived_back = exchange(adjoint_part.reshape(places, share, STATE))
    grad_out_weight = reduce_weight(dot(gated_low, cotangent, (0, 0)))
    grad_in_gate = reduce_weight(dot(normed_low, grad_gate, (0, 0)))
    output = (hidden_f + dot(gated_low, weight_out)).astype(bf16)
    u_inner, dbc = call(
        inner_back_kernel,
        [((rows, INNER), f32), ((rows, 2 * STATE), f32)],
        act, xw, g, cum, cum_t,
    )
    adjoint = exchange(running(arrived_back, factors, True)).reshape(INNER, STATE)
    grad_act, diff, col_state, direct = pl.pallas_call(
        outer_back_kernel,
        out_shape=[
            jax.ShapeDtypeStruct((rows, CONV_CH), bf16),
            jax.ShapeDtypeStruct((rows, 128), f32),
            jax.ShapeDtypeStruct((rows, 128), f32),
            jax.ShapeDtypeStruct((rows, 128), f32),
        ],
        in_specs=[whole] * 12,
        out_specs=[whole] * 4,
        scratch_shapes=[pltpu.VMEM((rows, INNER), f32)] * 3,
        compiler_params=pltpu.CompilerParams(vmem_limit_bytes=48 * 1024 * 1024),
    )(act, xw, xs, g, inner, u_inner, adjoint, step, tail, skip_wide, dbc, dc_state)

    sig = jax.nn.sigmoid(conv_out)
    grad_conv = grad_act.astype(f32) * (sig * (1.0 + conv_out * (1.0 - sig)))
    after = shifted(grad_conv[:HALO], SEQ_AXES, -1)
    across = jnp.exp(last[0]) * jnp.sum(
        (adjoint.astype(f32) * carry.astype(f32)).reshape(HEADS, HEADDIM * STATE), axis=1
    )
    upper = (col_ids >= row_ids).astype(f32)
    strict = (col_ids < row_ids).astype(f32)
    grad_log = (
        dot(upper, (diff + row_state)[:, :HEADS], precision=highest)
        + dot(strict, col_state[:, :HEADS], precision=highest)
        + across
    )
    grad_dt = (direct[:, :HEADS] - rate * grad_log) * jax.nn.sigmoid(dt_in)
    grad_a_log = jnp.sum(grad_log * log_decay, axis=0)
    grad_dt_bias = jnp.sum(grad_dt, axis=0)
    grad_skip = jnp.sum(gskip.reshape(HEADS, HEADDIM), axis=1)

    grad_ext = jnp.concatenate([grad_conv, after], axis=0)
    grad_conv_in = conv_weight[CONV - 1] * grad_ext[0:rows]
    for k in range(CONV - 1):
        grad_conv_in = grad_conv_in + conv_weight[k] * grad_ext[CONV - 1 - k : CONV - 1 - k + rows]
    grad_cb = jnp.sum(grad_conv, axis=0)
    grad_cw = jnp.stack(
        [jnp.sum(grad_conv * extended[k : k + rows], axis=0) for k in range(CONV)]
    )
    grad_rest = jnp.concatenate([grad_conv_in, grad_dt], axis=1).astype(bf16)
    grad_in_rest = reduce_weight(dot(normed_low, grad_rest, (0, 0)))
    grad_normed = dot(grad_gate, weight_gate, (1, 1)) + dot(grad_rest, weight_conv, (1, 1))
    pulled = grad_normed * norm_gain
    grad_hidden = (
        cotangent.astype(f32)
        + r1 * pulled
        - r1 * r1 * r1 * hidden_f * jnp.mean(pulled * hidden_f, axis=-1, keepdims=True)
    )
    grad_ngain = jnp.sum(grad_normed * hidden_f * r1, axis=0)
    grad_in_weight = jnp.concatenate([grad_in_gate, grad_in_rest], axis=1)
    small = [grad_ngain, grad_cw.reshape(-1), grad_cb, grad_dt_bias, grad_a_log, grad_skip, ggain[0]]
    packed = jnp.concatenate(small)
    size = packed.shape[0]
    packed = jnp.pad(packed, (0, -size % 1024)).reshape(-1, 128)
    total = jnp.sum(lax.all_gather(packed, ("dp", "ctx", "head")), axis=0).reshape(-1)
    sums, start = [], 0
    for part in small:
        sums.append(total[start : start + part.shape[0]])
        start += part.shape[0]
    return (
        output,
        grad_hidden,
        sums[0],
        grad_in_weight,
        sums[1].reshape(CONV, CONV_CH),
        sums[2],
        sums[3],
        sums[4],
        sums[5],
        sums[6],
        grad_out_weight,
    )


def solution(mesh):
    return jax.shard_map(
        body,
        mesh=mesh,
        in_specs=(
            P(("dp", "ctx", "head"), None),
            P(),
            P(("dp", "ctx"), None),
            P(),
            P(),
            P(),
            P(),
            P(),
            P(),
            P(("dp", "ctx"), None),
            P(("dp", "ctx", "head"), None),
        ),
        out_specs=(
            P(("dp", "ctx", "head"), None),
            P(("dp", "ctx", "head"), None),
            P(),
            P(("dp", "ctx"), None),
            P(),
            P(),
            P(),
            P(),
            P(),
            P(),
            P(("dp", "ctx"), None),
        ),
        check_vma=False,
    )
```

```python
import jax
import jax.numpy as jnp
from jax import lax
from jax.experimental import pallas as pl
from jax.experimental.pallas import tpu as pltpu
from jax.sharding import PartitionSpec as P

HEADS = 24
HEADDIM = 64
STATE = 128
CONV = 4
INNER = 1536
CONV_CH = 1792
PAIRS = HEADS // 2
PAIR = 2 * HEADDIM
HALO = 8

epsilon = 1e-05
highest = lax.Precision.HIGHEST
f32 = jnp.float32
bf16 = jnp.bfloat16
WEIGHT_AXES = ("dp", "ctx")
SEQ_AXES = ("ctx", "head")


def dot(a, b, dims=(1, 0), **more):
    return lax.dot_general(
        a, b, (((dims[0],), (dims[1],)), ((), ())), preferred_element_type=f32, **more
    )


def pair_columns(p):
    return slice(p * PAIR, (p + 1) * PAIR)


def low_lanes(rows):
    return lax.broadcasted_iota(jnp.int32, (rows, PAIR), 1) < HEADDIM


def spread_pair(values, p, first):
    return jnp.where(first, values[:, 2 * p : 2 * p + 1], values[:, 2 * p + 1 : 2 * p + 2])


def head_selector():
    rows = lax.broadcasted_iota(jnp.int32, (INNER, 128), 0) // HEADDIM
    cols = lax.broadcasted_iota(jnp.int32, (INNER, 128), 1)
    return (rows == cols).astype(f32)


def call(kernel, outs, *args):
    whole = pl.BlockSpec(memory_space=pltpu.VMEM)
    return pl.pallas_call(
        kernel,
        out_shape=[jax.ShapeDtypeStruct(s, d) for s, d in outs],
        in_specs=[whole] * len(args),
        out_specs=[whole] * len(outs),
        compiler_params=pltpu.CompilerParams(vmem_limit_bytes=48 * 1024 * 1024),
    )(*args)


def state_kernel(act, step, tail, xw_out, xs_out, state_out):
    rows = act.shape[0]
    first = low_lanes(rows)
    step_v, tail_v = step[...], tail[...]
    b_rows = act[:, INNER : INNER + STATE]
    for p in range(PAIRS):
        cols = pair_columns(p)
        weighted = act[:, cols].astype(f32) * spread_pair(step_v, p, first)
        xw_out[:, cols] = weighted.astype(bf16)
        tailed = (weighted * spread_pair(tail_v, p, first)).astype(bf16)
        xs_out[:, cols] = tailed
        state_out[cols, :] = dot(tailed, b_rows, (0, 0)).astype(bf16)


def decay_matrix(cum_v, cum_rows, h, causal):
    spread = cum_v[:, h : h + 1] - cum_rows[h : h + 1, :]
    return jnp.exp(jnp.where(causal, spread, -1e30))


def causal_mask(rows):
    return lax.broadcasted_iota(jnp.int32, (rows, rows), 1) <= lax.broadcasted_iota(
        jnp.int32, (rows, rows), 0
    )


def inner_kernel(act, xw, cum, cum_t, y_out):
    rows = act.shape[0]
    first = low_lanes(rows)
    causal = causal_mask(rows)
    scores = dot(act[:, INNER + STATE :], act[:, INNER : INNER + STATE], (1, 1))
    cum_v, cum_rows = cum[...], cum_t[...]
    for p in range(PAIRS):
        cols = pair_columns(p)
        both = []
        for h in (2 * p, 2 * p + 1):
            weights = (decay_matrix(cum_v, cum_rows, h, causal) * scores).astype(bf16)
            both.append(dot(weights, xw[:, cols]))
        y_out[:, cols] = jnp.where(first, both[0], both[1])


def middle_kernel(
    act, inner, carry, grown, skip, gate, gain, grad_gn,
    gated_low_out, grad_gate_out, g_out, adjoint_out, ggain_out, skip_out, row_out, dc_out,
    gated_s, ystate_s,
):
    rows = act.shape[0]
    first = low_lanes(rows)
    grown_v = grown[...]
    c_rows = act[:, INNER + STATE :]
    square = jnp.zeros((rows, 1), f32)
    inner_product = jnp.zeros((rows, 1), f32)
    for p in range(PAIRS):
        cols = pair_columns(p)
        ystate = dot(c_rows, carry[cols, :], (1, 1)) * spread_pair(grown_v, p, first)
        ystate_s[:, cols] = ystate
        mixer = (inner[:, cols] + ystate + skip[:, cols] * act[:, cols].astype(f32)).astype(bf16)
        gate_f = gate[:, cols].astype(f32)
        gated = mixer.astype(f32) * (gate_f * jax.nn.sigmoid(gate_f))
        gated_s[:, cols] = gated
        g_out[:, cols] = mixer
        square = square + jnp.sum(gated * gated, axis=1, keepdims=True)
        inner_product = inner_product + jnp.sum(
            grad_gn[:, cols] * gain[:, cols] * gated, axis=1, keepdims=True
        )
    scale = lax.rsqrt(square * (1.0 / INNER) + epsilon)
    pull = scale * scale * scale * (inner_product * (1.0 / INNER))
    dc_total = jnp.zeros((rows, STATE), f32)
    row_total = jnp.zeros((rows, 128), f32)
    head_col = lax.broadcasted_iota(jnp.int32, (rows, 128), 1)
    for p in range(PAIRS):
        cols = pair_columns(p)
        gated = gated_s[:, cols]
        normal = gated * scale
        gated_low_out[:, cols] = (normal * gain[:, cols]).astype(bf16)
        grad_n = grad_gn[:, cols]
        ggain_out[:, cols] = jnp.sum(grad_n * normal, axis=0, keepdims=True)
        grad_gated = scale * (grad_n * gain[:, cols]) - pull * gated
        gate_f = gate[:, cols].astype(f32)
        sig = jax.nn.sigmoid(gate_f)
        mixer = g_out[:, cols].astype(f32)
        grad_gate_out[:, cols] = (
            grad_gated * mixer * (sig * (1.0 + gate_f * (1.0 - sig)))
        ).astype(bf16)
        g_low = (grad_gated * (gate_f * sig)).astype(bf16)
        g_out[:, cols] = g_low
        g_f = g_low.astype(f32)
        g_grown = (g_f * spread_pair(grown_v, p, first)).astype(bf16)
        adjoint_out[cols, :] = dot(g_grown, c_rows, (0, 0)).astype(bf16)
        dc_total = dc_total + dot(g_grown, carry[cols, :])
        skip_out[:, cols] = jnp.sum(g_f * act[:, cols].astype(f32), axis=0, keepdims=True)
        term = g_f * ystate_s[:, cols]
        for k in range(2):
            part = jnp.sum(jnp.where(first == (k == 0), term, 0.0), axis=1, keepdims=True)
            row_total = row_total + jnp.where(head_col == 2 * p + k, part, 0.0)
    dc_out[...] = dc_total
    row_out[...] = row_total


def inner_back_kernel(act, xw, g, cum, cum_t, u_out, dbc_out):
    rows = act.shape[0]
    first = low_lanes(rows)
    causal = causal_mask(rows)
    b_rows, c_rows = act[:, INNER : INNER + STATE], act[:, INNER + STATE :]
    scores = dot(c_rows, b_rows, (1, 1))
    cum_v, cum_rows = cum[...], cum_t[...]
    grad_scores = jnp.zeros((rows, rows), f32)
    zero = jnp.zeros((rows, PAIR), bf16)
    for p in range(PAIRS):
        cols = pair_columns(p)
        both = []
        for k in range(2):
            decays = decay_matrix(cum_v, cum_rows, 2 * p + k, causal)
            weights = (decays * scores).astype(bf16)
            both.append(dot(weights, g[:, cols], (0, 0)))
            own = jnp.where(first == (k == 0), g[:, cols], zero)
            grad_scores = grad_scores + decays * dot(own, xw[:, cols], (1, 1))
        u_out[:, cols] = jnp.where(first, both[0], both[1])
    low = grad_scores.astype(bf16)
    dbc_out[:, :STATE] = dot(low, c_rows, (0, 0))
    dbc_out[:, STATE:] = dot(low, b_rows)


def outer_back_kernel(
    act, xw, xs, g, inner, u_inner, adjoint, step, tail, skip, dbc, dc_state,
    grad_act_out, diff_out, col_out, direct_out, term_s, col_s, direct_s,
):
    rows = act.shape[0]
    first = low_lanes(rows)
    step_v, tail_v = step[...], tail[...]
    b_rows = act[:, INNER : INNER + STATE]
    db_total = dbc[:, :STATE]
    for p in range(PAIRS):
        cols = pair_columns(p)
        x_f = act[:, cols].astype(f32)
        g_f = g[:, cols].astype(f32)
        step_b = spread_pair(step_v, p, first)
        u_state = dot(b_rows, adjoint[cols, :], (1, 1)) * spread_pair(tail_v, p, first)
        u_in = u_inner[:, cols]
        u_all = u_in + u_state
        grad_act_out[:, cols] = (step_b * u_all + skip[:, cols] * g_f).astype(bf16)
        term_s[:, cols] = g_f * inner[:, cols] - xw[:, cols].astype(f32) * u_in
        col_s[:, cols] = step_b * x_f * u_state
        direct_s[:, cols] = x_f * u_all
        db_total = db_total + dot(xs[:, cols], adjoint[cols, :])
    grad_act_out[:, INNER : INNER + STATE] = db_total.astype(bf16)
    grad_act_out[:, INNER + STATE :] = (dbc[:, STATE:] + dc_state[...]).astype(bf16)
    selector = head_selector()
    diff_out[...] = dot(term_s[...], selector, precision=highest)
    col_out[...] = dot(col_s[...], selector, precision=highest)
    direct_out[...] = dot(direct_s[...], selector, precision=highest)


def shifted(value, axis, by):
    length = lax.axis_size(axis)
    pairs = [(i, i + by) for i in range(length) if 0 <= i + by < length]
    return lax.ppermute(value, axis, pairs)


def exchange(value):
    return lax.all_to_all(value, SEQ_AXES, split_axis=0, concat_axis=0, tiled=True)


def running(parts, factors, reverse):
    count = parts.shape[0]
    order = range(count - 1, -1, -1) if reverse else range(count)
    state = jnp.zeros(parts.shape[1:], f32)
    kept = [None] * count
    for i in order:
        kept[i] = state.astype(bf16)
        state = factors[i][:, None] * state + parts[i].astype(f32)
    return jnp.stack(kept)


def collect(value, axes):
    count = lax.axis_size(axes)
    wide = jnp.broadcast_to(value, (count,) + value.shape)
    return lax.all_to_all(wide, axes, split_axis=0, concat_axis=0, tiled=True)


def reduce_weight(part):
    shard = lax.psum_scatter(part.astype(bf16), WEIGHT_AXES, scatter_dimension=0, tiled=True)
    groups = lax.axis_size("head")
    pieces = lax.all_to_all(
        shard.reshape(groups, -1, shard.shape[1]), "head", split_axis=0, concat_axis=0, tiled=True
    )
    own = jnp.sum(pieces.astype(f32), axis=0).astype(bf16)
    return collect(own, "head").reshape(shard.shape).astype(f32)


def body(
    hidden,
    norm_gain,
    in_weight,
    conv_weight,
    conv_bias,
    dt_bias,
    a_log,
    skip_gain,
    gate_gain,
    out_weight,
    cotangent,
):
    rows = hidden.shape[0]
    places = lax.axis_size(SEQ_AXES)
    place = lax.axis_index(SEQ_AXES)
    weight_conv = lax.all_gather(in_weight[:, INNER:], WEIGHT_AXES, axis=0, tiled=True)
    before = shifted(hidden[rows - HALO :], SEQ_AXES, 1)
    owners = lax.axis_size(WEIGHT_AXES)
    width = out_weight.shape[1]
    half = out_weight.shape[0] // 2
    joined = jnp.concatenate(
        [in_weight[:, :INNER], out_weight[:half], out_weight[half:]], axis=1
    )
    gathered = lax.all_gather(joined, WEIGHT_AXES, axis=0, tiled=True)
    weight_gate = gathered[:, :INNER]
    weight_out = (
        gathered[:, INNER:].reshape(owners, half, 2, width).transpose(0, 2, 1, 3).reshape(INNER, width)
    )

    extended_f = jnp.concatenate([before, hidden], axis=0).astype(f32)
    variance = jnp.mean(extended_f * extended_f, axis=-1, keepdims=True)
    r1 = lax.rsqrt(variance + epsilon)
    normed_ext = (extended_f * r1 * norm_gain).astype(bf16)
    hidden_f, r1, normed_low = extended_f[HALO:], r1[HALO:], normed_ext[HALO:]

    projected = dot(normed_ext, weight_conv).astype(bf16)
    extended = projected[HALO - (CONV - 1) :, :CONV_CH].astype(f32)
    dt_in = projected[HALO:, CONV_CH:].astype(f32) + dt_bias
    conv_out = conv_bias + conv_weight[0] * extended[0:rows]
    for k in range(1, CONV):
        conv_out = conv_out + conv_weight[k] * extended[k : k + rows]
    act = (conv_out * jax.nn.sigmoid(conv_out)).astype(bf16)

    row_ids = lax.broadcasted_iota(jnp.int32, (rows, rows), 0)
    col_ids = lax.broadcasted_iota(jnp.int32, (rows, rows), 1)
    lower = (col_ids <= row_ids).astype(f32)
    rate = jnp.exp(a_log)
    step = jax.nn.softplus(dt_in)
    log_decay = -step * rate
    cum = dot(lower, log_decay, precision=highest)
    last = cum[rows - 1 :]
    tail = jnp.exp(last - cum)
    grown = jnp.exp(cum)
    cum_t = cum.T
    skip_wide = jnp.repeat(skip_gain, HEADDIM)[None]

    xw, xs, state = call(
        state_kernel,
        [((rows, INNER), bf16), ((rows, INNER), bf16), ((INNER, STATE), bf16)],
        act, step, tail,
    )
    share = INNER // places
    high = last.astype(bf16)
    rest = last - high.astype(f32)
    middle = rest.astype(bf16)
    lowest = (rest - middle.astype(f32)).astype(bf16)
    logs = jnp.pad(jnp.concatenate([high, middle, lowest], axis=0), ((0, 13), (0, STATE - HEADS)))
    sent = jnp.concatenate(
        [state.reshape(places, share, STATE), jnp.broadcast_to(logs, (places, 16, STATE))], axis=1
    )
    arrived = exchange(sent)
    inner = call(inner_kernel, [((rows, INNER), f32)], act, xw, cum, cum_t)[0]
    gate = dot(normed_low, weight_gate).astype(bf16)
    grad_gn = dot(cotangent, weight_out, (1, 1))

    all_logs = jnp.sum(arrived[:, share : share + 3, :HEADS].astype(f32), axis=1)
    owner = (place * share + jnp.arange(share)) // HEADDIM
    mine = (owner[None] == jnp.arange(HEADS)[:, None]).astype(f32)
    factors = dot(jnp.exp(all_logs), mine, precision=highest)
    carry = exchange(running(arrived[:, :share], factors, False)).reshape(INNER, STATE)

    middle_outs = [
        ((rows, INNER), bf16),
        ((rows, INNER), bf16),
        ((rows, INNER), bf16),
        ((INNER, STATE), bf16),
        ((1, INNER), f32),
        ((1, INNER), f32),
        ((rows, 128), f32),
        ((rows, STATE), f32),
    ]
    whole = pl.BlockSpec(memory_space=pltpu.VMEM)
    gated_low, grad_gate, g, adjoint_part, ggain, gskip, row_state, dc_state = pl.pallas_call(
        middle_kernel,
        out_shape=[jax.ShapeDtypeStruct(s, d) for s, d in middle_outs],
        in_specs=[whole] * 8,
        out_specs=[whole] * 8,
        scratch_shapes=[pltpu.VMEM((rows, INNER), f32)] * 2,
        compiler_params=pltpu.CompilerParams(vmem_limit_bytes=48 * 1024 * 1024),
    )(act, inner, carry, grown, skip_wide, gate, gate_gain[None], grad_gn)

    arrived_back = exchange(adjoint_part.reshape(places, share, STATE))
    out_part = dot(gated_low, cotangent, (0, 0)).astype(bf16).reshape(owners, 2, half, width)
    gate_terms = dot(normed_low, grad_gate, (0, 0)).astype(bf16).reshape(owners, half, INNER)
    early = jnp.concatenate([gate_terms, out_part[:, 0], out_part[:, 1]], axis=2)
    early = reduce_weight(early.reshape(owners * half, INNER + 2 * width))
    grad_in_gate = early[:, :INNER]
    grad_out_weight = jnp.concatenate(
        [early[:, INNER : INNER + width], early[:, INNER + width :]], axis=0
    )
    output = (hidden_f + dot(gated_low, weight_out)).astype(bf16)
    u_inner, dbc = call(
        inner_back_kernel,
        [((rows, INNER), f32), ((rows, 2 * STATE), f32)],
        act, xw, g, cum, cum_t,
    )
    adjoint = exchange(running(arrived_back, factors, True)).reshape(INNER, STATE)
    grad_act, diff, col_state, direct = pl.pallas_call(
        outer_back_kernel,
        out_shape=[
            jax.ShapeDtypeStruct((rows, CONV_CH), bf16),
            jax.ShapeDtypeStruct((rows, 128), f32),
            jax.ShapeDtypeStruct((rows, 128), f32),
            jax.ShapeDtypeStruct((rows, 128), f32),
        ],
        in_specs=[whole] * 12,
        out_specs=[whole] * 4,
        scratch_shapes=[pltpu.VMEM((rows, INNER), f32)] * 3,
        compiler_params=pltpu.CompilerParams(vmem_limit_bytes=48 * 1024 * 1024),
    )(act, xw, xs, g, inner, u_inner, adjoint, step, tail, skip_wide, dbc, dc_state)

    sig = jax.nn.sigmoid(conv_out)
    grad_conv = grad_act.astype(f32) * (sig * (1.0 + conv_out * (1.0 - sig)))
    after = shifted(grad_conv[:HALO], SEQ_AXES, -1)
    across = jnp.exp(last[0]) * jnp.sum(
        (adjoint.astype(f32) * carry.astype(f32)).reshape(HEADS, HEADDIM * STATE), axis=1
    )
    upper = (col_ids >= row_ids).astype(f32)
    strict = (col_ids < row_ids).astype(f32)
    grad_log = (
        dot(upper, (diff + row_state)[:, :HEADS], precision=highest)
        + dot(strict, col_state[:, :HEADS], precision=highest)
        + across
    )
    grad_dt = (direct[:, :HEADS] - rate * grad_log) * jax.nn.sigmoid(dt_in)
    grad_a_log = jnp.sum(grad_log * log_decay, axis=0)
    grad_dt_bias = jnp.sum(grad_dt, axis=0)
    grad_skip = jnp.sum(gskip.reshape(HEADS, HEADDIM), axis=1)

    grad_ext = jnp.concatenate([grad_conv, after], axis=0)
    grad_conv_in = conv_weight[CONV - 1] * grad_ext[0:rows]
    for k in range(CONV - 1):
        grad_conv_in = grad_conv_in + conv_weight[k] * grad_ext[CONV - 1 - k : CONV - 1 - k + rows]
    grad_cb = jnp.sum(grad_conv, axis=0)
    grad_cw = jnp.stack(
        [jnp.sum(grad_conv * extended[k : k + rows], axis=0) for k in range(CONV)]
    )
    grad_rest = jnp.concatenate([grad_conv_in, grad_dt], axis=1).astype(bf16)
    grad_in_rest = reduce_weight(dot(normed_low, grad_rest, (0, 0)))
    grad_normed = dot(grad_gate, weight_gate, (1, 1)) + dot(grad_rest, weight_conv, (1, 1))
    pulled = grad_normed * norm_gain
    grad_hidden = (
        cotangent.astype(f32)
        + r1 * pulled
        - r1 * r1 * r1 * hidden_f * jnp.mean(pulled * hidden_f, axis=-1, keepdims=True)
    )
    grad_ngain = jnp.sum(grad_normed * hidden_f * r1, axis=0)
    grad_in_weight = jnp.concatenate([grad_in_gate, grad_in_rest], axis=1)
    small = [grad_ngain, grad_cw.reshape(-1), grad_cb, grad_dt_bias, grad_a_log, grad_skip, ggain[0]]
    packed = jnp.concatenate(small)
    size = packed.shape[0]
    packed = jnp.pad(packed, (0, -size % 1024)).reshape(-1, 128)
    total = jnp.sum(collect(packed, WEIGHT_AXES), axis=0)
    total = jnp.sum(collect(total, "head"), axis=0).reshape(-1)
    sums, start = [], 0
    for part in small:
        sums.append(total[start : start + part.shape[0]])
        start += part.shape[0]
    return (
        output,
        grad_hidden,
        sums[0],
        grad_in_weight,
        sums[1].reshape(CONV, CONV_CH),
        sums[2],
        sums[3],
        sums[4],
        sums[5],
        sums[6],
        grad_out_weight,
    )


def solution(mesh):
    return jax.shard_map(
        body,
        mesh=mesh,
        in_specs=(
            P(("dp", "ctx", "head"), None),
            P(),
            P(("dp", "ctx"), None),
            P(),
            P(),
            P(),
            P(),
            P(),
            P(),
            P(("dp", "ctx"), None),
            P(("dp", "ctx", "head"), None),
        ),
        out_specs=(
            P(("dp", "ctx", "head"), None),
            P(("dp", "ctx", "head"), None),
            P(),
            P(("dp", "ctx"), None),
            P(),
            P(),
            P(),
            P(),
            P(),
            P(),
            P(("dp", "ctx"), None),
        ),
        check_vma=False,
    )
```

```python
import functools

import jax
import jax.numpy as jnp
from jax import lax
from jax.experimental import pallas as pl
from jax.experimental.pallas import tpu as pltpu
from jax.sharding import PartitionSpec as P

HEADS = 24
HEADDIM = 64
STATE = 128
CONV = 4
INNER = 1536
CONV_CH = 1792
PAIRS = HEADS // 2
PAIR = 2 * HEADDIM
HALO = 8

epsilon = 1e-05
highest = lax.Precision.HIGHEST
f32 = jnp.float32
bf16 = jnp.bfloat16
WEIGHT_AXES = ("dp", "ctx")
SEQ_AXES = ("ctx", "head")


def dot(a, b, dims=(1, 0), **more):
    return lax.dot_general(
        a, b, (((dims[0],), (dims[1],)), ((), ())), preferred_element_type=f32, **more
    )


def pair_columns(p):
    return slice(p * PAIR, (p + 1) * PAIR)


def low_lanes(rows):
    return lax.broadcasted_iota(jnp.int32, (rows, PAIR), 1) < HEADDIM


def spread_pair(values, p, first):
    return jnp.where(first, values[:, 2 * p : 2 * p + 1], values[:, 2 * p + 1 : 2 * p + 2])


def head_selector():
    rows = lax.broadcasted_iota(jnp.int32, (INNER, 128), 0) // HEADDIM
    cols = lax.broadcasted_iota(jnp.int32, (INNER, 128), 1)
    return (rows == cols).astype(f32)


def call(kernel, outs, *args):
    whole = pl.BlockSpec(memory_space=pltpu.VMEM)
    return pl.pallas_call(
        kernel,
        out_shape=[jax.ShapeDtypeStruct(s, d) for s, d in outs],
        in_specs=[whole] * len(args),
        out_specs=[whole] * len(outs),
        compiler_params=pltpu.CompilerParams(vmem_limit_bytes=48 * 1024 * 1024),
    )(*args)


def state_kernel(act, step, tail, xw_out, xs_out, state_out):
    rows = act.shape[0]
    first = low_lanes(rows)
    step_v, tail_v = step[...], tail[...]
    b_rows = act[:, INNER : INNER + STATE]
    for p in range(PAIRS):
        cols = pair_columns(p)
        weighted = act[:, cols].astype(f32) * spread_pair(step_v, p, first)
        xw_out[:, cols] = weighted.astype(bf16)
        tailed = (weighted * spread_pair(tail_v, p, first)).astype(bf16)
        xs_out[:, cols] = tailed
        state_out[cols, :] = dot(tailed, b_rows, (0, 0)).astype(bf16)


def decay_matrix(cum_v, cum_rows, h, causal):
    spread = cum_v[:, h : h + 1] - cum_rows[h : h + 1, :]
    return jnp.exp(jnp.where(causal, spread, -1e30))


def causal_mask(rows):
    return lax.broadcasted_iota(jnp.int32, (rows, rows), 1) <= lax.broadcasted_iota(
        jnp.int32, (rows, rows), 0
    )


def inner_kernel(act, xw, cum, cum_t, y_out):
    rows = act.shape[0]
    first = low_lanes(rows)
    causal = causal_mask(rows)
    scores = dot(act[:, INNER + STATE :], act[:, INNER : INNER + STATE], (1, 1))
    cum_v, cum_rows = cum[...], cum_t[...]
    for p in range(PAIRS):
        cols = pair_columns(p)
        both = []
        for h in (2 * p, 2 * p + 1):
            weights = (decay_matrix(cum_v, cum_rows, h, causal) * scores).astype(bf16)
            both.append(dot(weights, xw[:, cols]))
        y_out[:, cols] = jnp.where(first, both[0], both[1])


def middle_kernel(
    act, inner, carry, grown, skip, gate, gain, grad_gn,
    gated_low_out, grad_gate_out, g_out, adjoint_out, ggain_out, skip_out, row_out, dc_out,
    gated_s, ystate_s,
):
    rows = act.shape[0]
    first = low_lanes(rows)
    grown_v = grown[...]
    c_rows = act[:, INNER + STATE :]
    square = jnp.zeros((rows, 1), f32)
    inner_product = jnp.zeros((rows, 1), f32)
    for p in range(PAIRS):
        cols = pair_columns(p)
        ystate = dot(c_rows, carry[cols, :], (1, 1)) * spread_pair(grown_v, p, first)
        ystate_s[:, cols] = ystate
        mixer = (inner[:, cols] + ystate + skip[:, cols] * act[:, cols].astype(f32)).astype(bf16)
        gate_f = gate[:, cols].astype(f32)
        gated = mixer.astype(f32) * (gate_f * jax.nn.sigmoid(gate_f))
        gated_s[:, cols] = gated
        g_out[:, cols] = mixer
        square = square + jnp.sum(gated * gated, axis=1, keepdims=True)
        inner_product = inner_product + jnp.sum(
            grad_gn[:, cols] * gain[:, cols] * gated, axis=1, keepdims=True
        )
    scale = lax.rsqrt(square * (1.0 / INNER) + epsilon)
    pull = scale * scale * scale * (inner_product * (1.0 / INNER))
    dc_total = jnp.zeros((rows, STATE), f32)
    row_total = jnp.zeros((rows, 128), f32)
    head_col = lax.broadcasted_iota(jnp.int32, (rows, 128), 1)
    for p in range(PAIRS):
        cols = pair_columns(p)
        gated = gated_s[:, cols]
        normal = gated * scale
        gated_low_out[:, cols] = (normal * gain[:, cols]).astype(bf16)
        grad_n = grad_gn[:, cols]
        ggain_out[:, cols] = jnp.sum(grad_n * normal, axis=0, keepdims=True)
        grad_gated = scale * (grad_n * gain[:, cols]) - pull * gated
        gate_f = gate[:, cols].astype(f32)
        sig = jax.nn.sigmoid(gate_f)
        mixer = g_out[:, cols].astype(f32)
        grad_gate_out[:, cols] = (
            grad_gated * mixer * (sig * (1.0 + gate_f * (1.0 - sig)))
        ).astype(bf16)
        g_low = (grad_gated * (gate_f * sig)).astype(bf16)
        g_out[:, cols] = g_low
        g_f = g_low.astype(f32)
        g_grown = (g_f * spread_pair(grown_v, p, first)).astype(bf16)
        adjoint_out[cols, :] = dot(g_grown, c_rows, (0, 0)).astype(bf16)
        dc_total = dc_total + dot(g_grown, carry[cols, :])
        skip_out[:, cols] = jnp.sum(g_f * act[:, cols].astype(f32), axis=0, keepdims=True)
        term = g_f * ystate_s[:, cols]
        for k in range(2):
            part = jnp.sum(jnp.where(first == (k == 0), term, 0.0), axis=1, keepdims=True)
            row_total = row_total + jnp.where(head_col == 2 * p + k, part, 0.0)
    dc_out[...] = dc_total
    row_out[...] = row_total


def inner_back_kernel(act, xw, g, cum, cum_t, u_out, dbc_out):
    rows = act.shape[0]
    first = low_lanes(rows)
    causal = causal_mask(rows)
    b_rows, c_rows = act[:, INNER : INNER + STATE], act[:, INNER + STATE :]
    scores = dot(c_rows, b_rows, (1, 1))
    cum_v, cum_rows = cum[...], cum_t[...]
    grad_scores = jnp.zeros((rows, rows), f32)
    zero = jnp.zeros((rows, PAIR), bf16)
    for p in range(PAIRS):
        cols = pair_columns(p)
        both = []
        for k in range(2):
            decays = decay_matrix(cum_v, cum_rows, 2 * p + k, causal)
            weights = (decays * scores).astype(bf16)
            both.append(dot(weights, g[:, cols], (0, 0)))
            own = jnp.where(first == (k == 0), g[:, cols], zero)
            grad_scores = grad_scores + decays * dot(own, xw[:, cols], (1, 1))
        u_out[:, cols] = jnp.where(first, both[0], both[1])
    low = grad_scores.astype(bf16)
    dbc_out[:, :STATE] = dot(low, c_rows, (0, 0))
    dbc_out[:, STATE:] = dot(low, b_rows)


def outer_back_kernel(
    act, xw, xs, g, inner, u_inner, adjoint, step, tail, skip, dbc, dc_state,
    grad_act_out, diff_out, col_out, direct_out, term_s, col_s, direct_s,
):
    rows = act.shape[0]
    first = low_lanes(rows)
    step_v, tail_v = step[...], tail[...]
    b_rows = act[:, INNER : INNER + STATE]
    db_total = dbc[:, :STATE]
    for p in range(PAIRS):
        cols = pair_columns(p)
        x_f = act[:, cols].astype(f32)
        g_f = g[:, cols].astype(f32)
        step_b = spread_pair(step_v, p, first)
        u_state = dot(b_rows, adjoint[cols, :], (1, 1)) * spread_pair(tail_v, p, first)
        u_in = u_inner[:, cols]
        u_all = u_in + u_state
        grad_act_out[:, cols] = (step_b * u_all + skip[:, cols] * g_f).astype(bf16)
        term_s[:, cols] = g_f * inner[:, cols] - xw[:, cols].astype(f32) * u_in
        col_s[:, cols] = step_b * x_f * u_state
        direct_s[:, cols] = x_f * u_all
        db_total = db_total + dot(xs[:, cols], adjoint[cols, :])
    grad_act_out[:, INNER : INNER + STATE] = db_total.astype(bf16)
    grad_act_out[:, INNER + STATE :] = (dbc[:, STATE:] + dc_state[...]).astype(bf16)
    selector = head_selector()
    diff_out[...] = dot(term_s[...], selector, precision=highest)
    col_out[...] = dot(col_s[...], selector, precision=highest)
    direct_out[...] = dot(direct_s[...], selector, precision=highest)


def shifted(value, axis, by):
    length = lax.axis_size(axis)
    pairs = [(i, i + by) for i in range(length) if 0 <= i + by < length]
    return lax.ppermute(value, axis, pairs)


def exchange(value):
    return lax.all_to_all(value, SEQ_AXES, split_axis=0, concat_axis=0, tiled=True)


def running_kernel(reverse, parts, decays, mine, out):
    count = parts.shape[0]
    chosen = mine[...]
    state = jnp.zeros(parts.shape[1:], f32)
    for i in range(count - 1, -1, -1) if reverse else range(count):
        out[i] = state.astype(bf16)
        factor = jnp.sum(chosen * decays[i], axis=1, keepdims=True)
        state = factor * state + parts[i].astype(f32)


def running(parts, decays, mine, reverse):
    kernel = functools.partial(running_kernel, reverse)
    return call(kernel, [(parts.shape, bf16)], parts, decays, mine)[0]


def collect(value, axes):
    count = lax.axis_size(axes)
    wide = jnp.broadcast_to(value, (count,) + value.shape)
    return lax.all_to_all(wide, axes, split_axis=0, concat_axis=0, tiled=True)


def scatter_weight(part):
    return lax.psum_scatter(part, WEIGHT_AXES, scatter_dimension=0, tiled=True)


def finish_weight(shard):
    groups = lax.axis_size("head")
    pieces = lax.all_to_all(
        shard.reshape(groups, -1, shard.shape[1]), "head", split_axis=0, concat_axis=0, tiled=True
    )
    own = jnp.sum(pieces.astype(f32), axis=0).astype(bf16)
    return collect(own, "head").reshape(shard.shape).astype(f32)


def body(
    hidden,
    norm_gain,
    in_weight,
    conv_weight,
    conv_bias,
    dt_bias,
    a_log,
    skip_gain,
    gate_gain,
    out_weight,
    cotangent,
):
    rows = hidden.shape[0]
    places = lax.axis_size(SEQ_AXES)
    place = lax.axis_index(SEQ_AXES)
    weight_conv = lax.all_gather(in_weight[:, INNER:], WEIGHT_AXES, axis=0, tiled=True)
    before = shifted(hidden[rows - HALO :], SEQ_AXES, 1)
    owners = lax.axis_size(WEIGHT_AXES)
    width = out_weight.shape[1]
    half = out_weight.shape[0] // 2
    joined = jnp.concatenate(
        [out_weight, in_weight[:, :width], in_weight[:, width:INNER]], axis=0
    )
    gathered = lax.all_gather(joined, WEIGHT_AXES)
    weight_out = gathered[:, : 2 * half].reshape(INNER, width)
    weight_left = gathered[:, 2 * half : 3 * half].reshape(width, width)
    weight_right = gathered[:, 3 * half :].reshape(width, width)

    extended_f = jnp.concatenate([before, hidden], axis=0).astype(f32)
    variance = jnp.mean(extended_f * extended_f, axis=-1, keepdims=True)
    r1 = lax.rsqrt(variance + epsilon)
    normed_ext = (extended_f * r1 * norm_gain).astype(bf16)
    hidden_f, r1, normed_low = extended_f[HALO:], r1[HALO:], normed_ext[HALO:]

    projected = dot(normed_ext, weight_conv).astype(bf16)
    extended = projected[HALO - (CONV - 1) :, :CONV_CH].astype(f32)
    dt_in = projected[HALO:, CONV_CH:].astype(f32) + dt_bias
    conv_out = conv_bias + conv_weight[0] * extended[0:rows]
    for k in range(1, CONV):
        conv_out = conv_out + conv_weight[k] * extended[k : k + rows]
    act = (conv_out * jax.nn.sigmoid(conv_out)).astype(bf16)

    row_ids = lax.broadcasted_iota(jnp.int32, (rows, rows), 0)
    col_ids = lax.broadcasted_iota(jnp.int32, (rows, rows), 1)
    lower = (col_ids <= row_ids).astype(f32)
    rate = jnp.exp(a_log)
    step = jax.nn.softplus(dt_in)
    log_decay = -step * rate
    cum = dot(lower, log_decay, precision=highest)
    last = cum[rows - 1 :]
    tail = jnp.exp(last - cum)
    grown = jnp.exp(cum)
    cum_t = cum.T
    skip_wide = jnp.repeat(skip_gain, HEADDIM)[None]

    xw, xs, state = call(
        state_kernel,
        [((rows, INNER), bf16), ((rows, INNER), bf16), ((INNER, STATE), bf16)],
        act, step, tail,
    )
    share = INNER // places
    high = last.astype(bf16)
    rest = last - high.astype(f32)
    middle = rest.astype(bf16)
    lowest = (rest - middle.astype(f32)).astype(bf16)
    logs = jnp.pad(jnp.concatenate([high, middle, lowest], axis=0), ((0, 13), (0, STATE - HEADS)))
    sent = jnp.concatenate(
        [state.reshape(places, share, STATE), jnp.broadcast_to(logs, (places, 16, STATE))], axis=1
    )
    arrived = exchange(sent)
    inner = call(inner_kernel, [((rows, INNER), f32)], act, xw, cum, cum_t)[0]
    gate = jnp.concatenate(
        [dot(normed_low, weight_left).astype(bf16), dot(normed_low, weight_right).astype(bf16)], axis=1
    )
    grad_gn = dot(cotangent, weight_out, (1, 1))

    decays = jnp.exp(
        jnp.sum(arrived[:, share : share + 3].astype(f32), axis=1, keepdims=True)
    )
    owner = (place * share + jnp.arange(share)) // HEADDIM
    mine = (owner[:, None] == jnp.arange(STATE)[None]).astype(f32)
    carry = exchange(running(arrived[:, :share], decays, mine, False)).reshape(INNER, STATE)

    middle_outs = [
        ((rows, INNER), bf16),
        ((rows, INNER), bf16),
        ((rows, INNER), bf16),
        ((INNER, STATE), bf16),
        ((1, INNER), f32),
        ((1, INNER), f32),
        ((rows, 128), f32),
        ((rows, STATE), f32),
    ]
    whole = pl.BlockSpec(memory_space=pltpu.VMEM)
    gated_low, grad_gate, g, adjoint_part, ggain, gskip, row_state, dc_state = pl.pallas_call(
        middle_kernel,
        out_shape=[jax.ShapeDtypeStruct(s, d) for s, d in middle_outs],
        in_specs=[whole] * 8,
        out_specs=[whole] * 8,
        scratch_shapes=[pltpu.VMEM((rows, INNER), f32)] * 2,
        compiler_params=pltpu.CompilerParams(vmem_limit_bytes=48 * 1024 * 1024),
    )(act, inner, carry, grown, skip_wide, gate, gate_gain[None], grad_gn)

    arrived_back = exchange(adjoint_part.reshape(places, share, STATE))
    out_part = dot(gated_low, cotangent, (0, 0)).astype(bf16).reshape(owners, 2 * half, width)
    left_part = dot(normed_low, grad_gate[:, :width], (0, 0)).astype(bf16)
    right_part = dot(normed_low, grad_gate[:, width:], (0, 0)).astype(bf16)
    early = jnp.concatenate(
        [out_part, left_part.reshape(owners, half, width), right_part.reshape(owners, half, width)],
        axis=1,
    ).reshape(owners * 4 * half, width)
    early, g_late = lax.optimization_barrier((early, g))
    early_shard = scatter_weight(early)
    output = (hidden_f + dot(gated_low, weight_out)).astype(bf16)
    u_inner, dbc = call(
        inner_back_kernel,
        [((rows, INNER), f32), ((rows, 2 * STATE), f32)],
        act, xw, g_late, cum, cum_t,
    )
    adjoint = exchange(running(arrived_back, decays, mine, True)).reshape(INNER, STATE)
    grad_act, diff, col_state, direct = pl.pallas_call(
        outer_back_kernel,
        out_shape=[
            jax.ShapeDtypeStruct((rows, CONV_CH), bf16),
            jax.ShapeDtypeStruct((rows, 128), f32),
            jax.ShapeDtypeStruct((rows, 128), f32),
            jax.ShapeDtypeStruct((rows, 128), f32),
        ],
        in_specs=[whole] * 12,
        out_specs=[whole] * 4,
        scratch_shapes=[pltpu.VMEM((rows, INNER), f32)] * 3,
        compiler_params=pltpu.CompilerParams(vmem_limit_bytes=48 * 1024 * 1024),
    )(act, xw, xs, g, inner, u_inner, adjoint, step, tail, skip_wide, dbc, dc_state)

    sig = jax.nn.sigmoid(conv_out)
    grad_conv = grad_act.astype(f32) * (sig * (1.0 + conv_out * (1.0 - sig)))
    after = shifted(grad_conv[:HALO], SEQ_AXES, -1)
    across = jnp.exp(last[0]) * jnp.sum(
        (adjoint.astype(f32) * carry.astype(f32)).reshape(HEADS, HEADDIM * STATE), axis=1
    )
    upper = (col_ids >= row_ids).astype(f32)
    strict = (col_ids < row_ids).astype(f32)
    grad_log = (
        dot(upper, (diff + row_state)[:, :HEADS], precision=highest)
        + dot(strict, col_state[:, :HEADS], precision=highest)
        + across
    )
    grad_dt = (direct[:, :HEADS] - rate * grad_log) * jax.nn.sigmoid(dt_in)
    grad_a_log = jnp.sum(grad_log * log_decay, axis=0)
    grad_dt_bias = jnp.sum(grad_dt, axis=0)
    grad_skip = jnp.sum(gskip.reshape(HEADS, HEADDIM), axis=1)

    grad_ext = jnp.concatenate([grad_conv, after], axis=0)
    grad_conv_in = conv_weight[CONV - 1] * grad_ext[0:rows]
    for k in range(CONV - 1):
        grad_conv_in = grad_conv_in + conv_weight[k] * grad_ext[CONV - 1 - k : CONV - 1 - k + rows]
    grad_cb = jnp.sum(grad_conv, axis=0)
    grad_cw = jnp.stack(
        [jnp.sum(grad_conv * extended[k : k + rows], axis=0) for k in range(CONV)]
    )
    grad_rest = jnp.concatenate([grad_conv_in, grad_dt], axis=1).astype(bf16)
    rest = dot(normed_low, grad_rest, (0, 0)).astype(bf16)
    early_shard, rest = lax.optimization_barrier((early_shard, rest))
    grad_in_rest = finish_weight(scatter_weight(rest))
    early_sum = finish_weight(early_shard)
    grad_out_weight = early_sum[: 2 * half]
    grad_in_gate = jnp.concatenate(
        [early_sum[2 * half : 3 * half], early_sum[3 * half :]], axis=1
    )
    grad_normed = (
        dot(grad_gate[:, :width], weight_left, (1, 1))
        + dot(grad_gate[:, width:], weight_right, (1, 1))
        + dot(grad_rest, weight_conv, (1, 1))
    )
    pulled = grad_normed * norm_gain
    grad_hidden = (
        cotangent.astype(f32)
        + r1 * pulled
        - r1 * r1 * r1 * hidden_f * jnp.mean(pulled * hidden_f, axis=-1, keepdims=True)
    )
    grad_ngain = jnp.sum(grad_normed * hidden_f * r1, axis=0)
    grad_in_weight = jnp.concatenate([grad_in_gate, grad_in_rest], axis=1)
    small = [grad_ngain, grad_cw.reshape(-1), grad_cb, grad_dt_bias, grad_a_log, grad_skip, ggain[0]]
    packed = jnp.concatenate(small)
    size = packed.shape[0]
    packed = jnp.pad(packed, (0, -size % 1024)).reshape(-1, 128)
    total = jnp.sum(collect(packed, WEIGHT_AXES), axis=0)
    total = jnp.sum(collect(total, "head"), axis=0).reshape(-1)
    sums, start = [], 0
    for part in small:
        sums.append(total[start : start + part.shape[0]])
        start += part.shape[0]
    return (
        output,
        grad_hidden,
        sums[0],
        grad_in_weight,
        sums[1].reshape(CONV, CONV_CH),
        sums[2],
        sums[3],
        sums[4],
        sums[5],
        sums[6],
        grad_out_weight,
    )


def solution(mesh):
    return jax.shard_map(
        body,
        mesh=mesh,
        in_specs=(
            P(("dp", "ctx", "head"), None),
            P(),
            P(("dp", "ctx"), None),
            P(),
            P(),
            P(),
            P(),
            P(),
            P(),
            P(("dp", "ctx"), None),
            P(("dp", "ctx", "head"), None),
        ),
        out_specs=(
            P(("dp", "ctx", "head"), None),
            P(("dp", "ctx", "head"), None),
            P(),
            P(("dp", "ctx"), None),
            P(),
            P(),
            P(),
            P(),
            P(),
            P(),
            P(("dp", "ctx"), None),
        ),
        check_vma=False,
    )
```
